1024 devices in a mesh: space: 256 (over z, y, core), mem: 4 (over x).
Axes of the slice: x: 4, y: 8, z: 16, core: 2. Of those that a mesh axis runs over, the one named last changes fastest.
Arguments:
- member_heat_solute: float32 [128, 2, 4096, 128], P('mem', None, 'space'), may hold values from -6 to 6
- velocity: float32 [128, 4096, 128], P('mem', 'space'), may hold values from 0.2 to 0.6
- phase_mask: int32 [4096, 128], P('space'), may hold values 0 or 1
- obs_index: int32 [4096], P('space'), may hold values from 0 to 2047
- obs_value: float32 [4096], P('space'), may hold values from -6 to 6
- obs_error: float32 [4096], P('space'), may hold values from 0.3 to 3
Outputs:
- analysis_hc: float32 [128, 2, 4096, 128], P('mem', None, 'space')
- analysis_velocity: float32 [128, 4096, 128], P('mem', 'space')
The draws below stay inside these ranges and needn't reach their ends.
Inputs may be any that keep to these rules, and one draw needn't show every extreme that they name: `obs_index`: observation o lies in slab o // 16; its entry counts cells row by row inside that slab.
All inputs are finite; a program needn't handle non-finite values. No bound on the sum of `phase_mask` on one device may be relied on, other than what follows from the above.
Results may differ from the reference program's by a relative error of at most 0.00015.
Values sent between devices are 32-bit elements; how exact they have to be, the bound alone decides.
No kernel may reach another device: no remote copies, remote signals or barrier semaphores. Data moves between devices by JAX's collectives and lax.ppermute only.
A program may use at most 32 MiB of HBM per device.

```python
import math
import jax
import jax.numpy as jnp
from jax import lax

ENS = 128
LZ = 16
W = 128
NOBS = 16
NZ = 4096
NOBS_ALL = 4096


def set_ends(array, own_key, least, high):
    extent = array.shape
    index_at = [jax.random.randint(jax.random.fold_in(own_key, axis), (), 0, extent[axis]) for axis in range(len(extent))]
    array = array.at[tuple(index_at)].set(least)
    longest = extent.index(max(extent))
    index_at[longest] = (index_at[longest] + 1) % extent[longest]
    return array.at[tuple(index_at)].set(high)


def shard_levels(own_key, dims, pieces, smallest, largest):
    def one(dim, shards_of):
        draws = jax.random.uniform(jax.random.fold_in(jax.random.fold_in(own_key, 6), dim), (shards_of,), jnp.float32, smallest / len(pieces), largest / len(pieces))
        return jnp.repeat(jnp.exp(draws), dims[dim] // shards_of).reshape((-1,) + (1,) * (len(dims) - dim - 1))

    factor_of = one(*pieces[0])
    for cut in pieces[1:]:
        factor_of = factor_of * one(*cut)
    return factor_of


def scatter_about(stream_key, dims, width, most, shards=(), kind=jnp.bfloat16):
    loudness = shard_levels(stream_key, dims, shards, -0.22, 0.18) if shards else 1.0
    values = jax.random.normal(stream_key, dims, jnp.float32) * width * loudness
    return jnp.minimum(jnp.maximum(values, -most), most).astype(kind)


def setup_inputs(seed: int = 0) -> dict:
    seeds = jax.random.split(jax.random.key(seed), 7)
    return {
        "member_heat_solute": scatter_about(seeds[0], (ENS, 2, NZ, W), 1.0, 6.0, ((0, 4), (2, 256)), jnp.float32),
        "velocity": jnp.clip(0.2 + 0.400000021 * jax.random.uniform(seeds[1], (ENS, NZ, W), jnp.float32) ** shard_levels(seeds[1], (ENS, NZ, W), ((0, 4), (1, 256)), -0.2, 0.2), 0.2, 0.6),
        "phase_mask": set_ends((jax.random.randint(seeds[2], (NZ, W), 0, 3) < 1).astype(jnp.int32), jax.random.fold_in(seeds[2], 1), 0, 1),
        "obs_index": set_ends(jax.random.randint(seeds[3], (NOBS_ALL,), 0, LZ * W), jax.random.fold_in(seeds[3], 1), 0, (LZ * W) - 1).astype(jnp.int32),
        "obs_value": scatter_about(seeds[4], (NOBS_ALL,), 1.0, 6.0, ((0, 256),), jnp.float32),
        "obs_error": jnp.clip(jnp.exp(math.log(3.0) - 2.3025851 * jax.random.uniform(seeds[5], (NOBS_ALL,), jnp.float32) ** shard_levels(seeds[5], (NOBS_ALL,), ((0, 256),), -0.2, 0.2)), 0.3, 3.0),
    }


heat_diffusion = 0.15
advection = 0.4
solute_diffusion = 0.05
segregation = 0.3
momentum_diffusion = 0.1
darcy_drag = 0.5
mushy_ratio = 1.0 / 3.0

def lateral(field):
    left = jnp.concatenate([field[..., :1], field[..., :-1]], axis=-1)
    right = jnp.concatenate([field[..., 1:], field[..., -1:]], axis=-1)
    return left + right - 2.0 * field

def advance(padded_heat, padded_temp, padded_solute, padded_speed, factor, mushy):
    heat = padded_heat[..., 1:-1, :]
    temp = padded_temp[..., 1:-1, :]
    solute = padded_solute[..., 1:-1, :]
    speed = padded_speed[..., 1:-1, :]
    temp_lap = padded_temp[..., 2:, :] + padded_temp[..., :-2, :] - 2.0 * temp + lateral(temp)
    solute_lap = padded_solute[..., 2:, :] + padded_solute[..., :-2, :] - 2.0 * solute + lateral(solute)
    speed_lap = padded_speed[..., 2:, :] + padded_speed[..., :-2, :] - 2.0 * speed + lateral(speed)
    new_heat = heat + heat_diffusion * temp_lap - advection * speed * (heat - padded_heat[..., :-2, :])
    new_solute = solute + solute_diffusion * solute_lap - advection * speed * (solute - padded_solute[..., :-2, :]) + segregation * mushy * (temp - solute)
    new_speed = speed + momentum_diffusion * speed_lap - darcy_drag * mushy * speed
    return (new_heat, new_solute, new_speed)

def pad_rows(field):
    return jnp.pad(field, ((1, 1), (0, 0)))

def analysis_weights(gram, project):
    members = gram.shape[0]
    ident = jnp.eye(members, dtype=jnp.float32)
    lower = jnp.linalg.cholesky(ident + gram)
    mean_offset = jax.scipy.linalg.cho_solve((lower, True), project)
    inverse_root = jax.scipy.linalg.solve_triangular(lower.T, ident, lower=False)
    center = ident - 1.0 / members
    combined = mean_offset[:, None] / jnp.sqrt(jnp.float32(members - 1)) + inverse_root
    return 1.0 / members + jnp.dot(center, combined, precision=lax.Precision.HIGHEST)

def reference(member_heat_solute, velocity, phase_mask, obs_index, obs_value, obs_error):
    mushy = phase_mask.astype(jnp.float32)
    factor = 1.0 - mushy * (1.0 - mushy_ratio)
    slab_of = (jnp.arange(NOBS_ALL, dtype=jnp.int32) // NOBS).astype(jnp.int32)
    global_index = (slab_of * (LZ * W) + obs_index).astype(jnp.int32)

    def single_member(inputs):
        pair, speed = inputs
        heat = pair[0]
        solute = pair[1]
        for section in range(2):
            temp = heat * factor
            heat, solute, speed = advance(pad_rows(heat), pad_rows(temp), pad_rows(solute), pad_rows(speed), factor, mushy)
        temp = heat * factor
        seen = temp.reshape(-1)[global_index]
        return (jnp.stack([heat, solute]), speed, seen)
    predicted_heat_solute, predicted_speed, measured_values = lax.map(single_member, (member_heat_solute, velocity))
    members = measured_values.shape[0]
    mean_obs = lax.optimization_barrier(jnp.mean(measured_values, axis=0))
    spread = (measured_values - mean_obs[None, :]).T / (obs_error[:, None] * jnp.sqrt(jnp.float32(members - 1)))
    innovation = (obs_value - mean_obs) / obs_error
    gram = jnp.dot(spread.T, spread, precision=lax.Precision.HIGHEST)
    project = jnp.dot(spread.T, innovation, precision=lax.Precision.HIGHEST)
    mixing = analysis_weights(gram, project)
    field_stack = jnp.concatenate([predicted_heat_solute, predicted_speed[:, None]], axis=1)
    flat = field_stack.reshape(members, -1)
    mixed = jnp.dot(mixing.T, flat, precision=lax.Precision.HIGHEST).reshape(field_stack.shape)
    return (mixed[:, :2], mixed[:, 2])
```

```python
import jax
import jax.numpy as jnp
from jax import lax
from jax.experimental import pallas as pl
from jax.experimental.pallas import tpu as pltpu
from jax.sharding import Mesh
from jax.sharding import PartitionSpec as P

heat_diffusion = 0.15
advection = 0.4
solute_diffusion = 0.05
segregation = 0.3
momentum_diffusion = 0.1
darcy_drag = 0.5
mushy_ratio = 1.0 / 3.0

SPACE = ("z", "y", "core")
HIGHEST = lax.Precision.HIGHEST


def lateral(field):
    left = jnp.concatenate([field[..., :1], field[..., :-1]], axis=-1)
    right = jnp.concatenate([field[..., 1:], field[..., -1:]], axis=-1)
    return left + right - 2.0 * field


def laplacian(padded):
    centre = padded[:, 1:-1]
    return padded[:, 2:] + padded[:, :-2] - 2.0 * centre + lateral(centre)


def advance(heat, solute, speed, mushy, factor):
    temp = heat * factor
    inner_heat = heat[:, 1:-1]
    inner_solute = solute[:, 1:-1]
    inner_speed = speed[:, 1:-1]
    inner_mushy = mushy[1:-1]
    carried = advection * inner_speed
    new_heat = (
        inner_heat + heat_diffusion * laplacian(temp) - carried * (inner_heat - heat[:, :-2])
    )
    new_solute = (
        inner_solute
        + solute_diffusion * laplacian(solute)
        - carried * (inner_solute - solute[:, :-2])
        + segregation * inner_mushy * (temp[:, 1:-1] - inner_solute)
    )
    new_speed = (
        inner_speed
        + momentum_diffusion * laplacian(speed)
        - darcy_drag * inner_mushy * inner_speed
    )
    return new_heat, new_solute, new_speed


def shared(value, axes):
    count = lax.axis_size(axes)
    return lax.all_to_all(
        jnp.broadcast_to(value[None], (count,) + value.shape), axes, 0, 0
    )


def weights_kernel(gram_ref, project_ref, out_ref, left, right):
    members = gram_ref.shape[0]
    rows = lax.broadcasted_iota(jnp.int32, (members, members), 0)
    cols = lax.broadcasted_iota(jnp.int32, (members, members), 1)
    ident = jnp.where(rows == cols, 1.0, 0.0)
    left[0:members, :] = gram_ref[...] + ident
    right[0:members, :] = ident
    left[members:, :] = jnp.broadcast_to(project_ref[...], (8, members))
    right[members:, :] = jnp.zeros((8, members), jnp.float32)
    total = members + 8
    for j in range(members):
        base = (j // 8) * 8
        row_a = left[j : j + 1, :]
        row_m = right[j : j + 1, :]
        pivot = lax.rsqrt(row_a[:, j : j + 1])
        scaled_a = row_a * pivot
        scaled_m = row_m * pivot
        column = left[base:total, j : j + 1] * pivot
        position = lax.broadcasted_iota(jnp.int32, (total - base, 1), 0) + base
        column = jnp.where(position > j, column, 0.0)
        left[base:total, :] = left[base:total, :] - column * scaled_a
        right[base:total, :] = right[base:total, :] - column * scaled_m
        right[j : j + 1, :] = scaled_m
    shift = -right[members : members + 1, :]
    combined = right[0:members, :] + shift * (1.0 / (members - 1) ** 0.5)
    mean = jnp.sum(combined, axis=1, keepdims=True) * (1.0 / members)
    out_ref[...] = combined - mean + 1.0 / members


def analysis_weights(gram, project):
    members = gram.shape[0]
    return pl.pallas_call(
        weights_kernel,
        out_shape=jax.ShapeDtypeStruct((members, members), jnp.float32),
        scratch_shapes=[
            pltpu.VMEM((members + 8, members), jnp.float32),
            pltpu.VMEM((members + 8, members), jnp.float32),
        ],
    )(gram, project)


def on_device(member_heat_solute, velocity, phase_mask, obs_index, obs_value, obs_error):
    members, _, depth, width = member_heat_solute.shape
    mushy = phase_mask.astype(jnp.float32)
    fields = jnp.concatenate(
        [
            member_heat_solute[:, 0],
            member_heat_solute[:, 1],
            velocity,
            mushy[None],
        ],
        axis=0,
    )
    count = lax.axis_size(SPACE)
    position = lax.axis_index(SPACE)
    above = lax.ppermute(fields[:, -2:], SPACE, [(i, i + 1) for i in range(count - 1)])
    below = lax.ppermute(fields[:, :2], SPACE, [(i + 1, i) for i in range(count - 1)])
    padded = jnp.concatenate([above, fields, below], axis=1)
    mushy = padded[3 * members]
    factor = 1.0 - mushy * (1.0 - mushy_ratio)
    heat = padded[:members]
    solute = padded[members : 2 * members]
    speed = padded[2 * members : 3 * members]
    heat, solute, speed = advance(heat, solute, speed, mushy, factor)
    row = lax.broadcasted_iota(jnp.int32, (depth + 2, 1), 0)
    outside = ((row == 0) & (position == 0)) | ((row == depth + 1) & (position == count - 1))
    heat = jnp.where(outside, 0.0, heat)
    solute = jnp.where(outside, 0.0, solute)
    speed = jnp.where(outside, 0.0, speed)
    heat, solute, speed = advance(heat, solute, speed, mushy[1:-1], factor[1:-1])

    temp = heat * factor[2:-2]
    flat_temp = temp.reshape(members, -1)
    cell_ids = jnp.arange(flat_temp.shape[1], dtype=jnp.int32)
    selector = jnp.where(obs_index[:, None] == cell_ids[None, :], 1.0, 0.0).astype(jnp.float32)
    observed_own = jnp.dot(selector, flat_temp.T, precision=HIGHEST)
    message = jnp.concatenate([observed_own, obs_value[:, None], obs_error[:, None]], axis=1)
    arrived = shared(message, ("y", "core", "mem"))
    mem_size = lax.axis_size("mem")
    slabs = arrived.shape[0] // mem_size
    n_obs = message.shape[0]
    arrived = arrived.reshape(slabs, mem_size, n_obs, members + 2)
    ensemble = mem_size * members
    measured = arrived[..., :members].transpose(0, 2, 1, 3).reshape(slabs * n_obs, ensemble)
    value = arrived[:, 0, :, members].reshape(slabs * n_obs)
    error = arrived[:, 0, :, members + 1].reshape(slabs * n_obs)
    mean_obs = jnp.mean(measured, axis=1)
    spread = (measured - mean_obs[:, None]) / (
        error[:, None] * jnp.sqrt(jnp.float32(ensemble - 1))
    )
    innovation = (value - mean_obs) / error
    pieces = mem_size * lax.axis_size("core")
    piece = lax.axis_index("mem") * lax.axis_size("core") + lax.axis_index("core")
    height = ensemble // pieces
    own_cols = lax.dynamic_slice_in_dim(spread, piece * height, height, 1)
    left = jnp.concatenate([own_cols, innovation[:, None]], axis=1)
    part = lax.dot_general(left, spread, (((0,), (0,)), ((), ())), precision=HIGHEST)
    part = jnp.sum(shared(part, "z"), axis=0)
    project = part[height:]
    gram = shared(part[:height], ("mem", "core")).reshape(ensemble, ensemble)
    weights = analysis_weights(gram, project)

    mem_index = lax.axis_index("mem")
    weights = lax.dynamic_slice_in_dim(weights, mem_index * members, members, 0)
    states = jnp.stack([heat, solute, speed], axis=1)
    result = None
    for step in range(mem_size):
        if step:
            source = lax.ppermute(
                states, "mem", [(i, (i + step) % mem_size) for i in range(mem_size)]
            )
        else:
            source = states
        origin = (mem_index - step + mem_size) % mem_size
        block = lax.dynamic_slice_in_dim(weights, origin * members, members, 1)
        term = jnp.einsum("kfzw,jk->jfzw", source, block, precision=HIGHEST)
        result = term if result is None else result + term
    return (result[:, :2], result[:, 2])


def solution(mesh):
    shaped = Mesh(mesh.devices.reshape(16, 8, 2, 4), ("z", "y", "core", "mem"))
    return jax.shard_map(
        on_device,
        mesh=shaped,
        in_specs=(
            P("mem", None, SPACE, None),
            P("mem", SPACE, None),
            P(SPACE, None),
            P(SPACE),
            P(SPACE),
            P(SPACE),
        ),
        out_specs=(P("mem", None, SPACE, None), P("mem", SPACE, None)),
        check_vma=False,
    )
```

```python
import jax
import jax.numpy as jnp
from jax import lax
from jax.experimental import pallas as pl
from jax.experimental.pallas import tpu as pltpu
from jax.sharding import Mesh
from jax.sharding import PartitionSpec as P

heat_diffusion = 0.15
advection = 0.4
solute_diffusion = 0.05
segregation = 0.3
momentum_diffusion = 0.1
darcy_drag = 0.5
mushy_ratio = 1.0 / 3.0

SPACE = ("z", "y", "core")
HIGHEST = lax.Precision.HIGHEST


def lateral(field):
    left = jnp.concatenate([field[..., :1], field[..., :-1]], axis=-1)
    right = jnp.concatenate([field[..., 1:], field[..., -1:]], axis=-1)
    return left + right - 2.0 * field


def laplacian(padded):
    centre = padded[:, 1:-1]
    return padded[:, 2:] + padded[:, :-2] - 2.0 * centre + lateral(centre)


def advance(heat, solute, speed, mushy, factor):
    temp = heat * factor
    inner_heat = heat[:, 1:-1]
    inner_solute = solute[:, 1:-1]
    inner_speed = speed[:, 1:-1]
    inner_mushy = mushy[1:-1]
    carried = advection * inner_speed
    new_heat = (
        inner_heat + heat_diffusion * laplacian(temp) - carried * (inner_heat - heat[:, :-2])
    )
    new_solute = (
        inner_solute
        + solute_diffusion * laplacian(solute)
        - carried * (inner_solute - solute[:, :-2])
        + segregation * inner_mushy * (temp[:, 1:-1] - inner_solute)
    )
    new_speed = (
        inner_speed
        + momentum_diffusion * laplacian(speed)
        - darcy_drag * inner_mushy * inner_speed
    )
    return new_heat, new_solute, new_speed


def shared(value, axes):
    count = lax.axis_size(axes)
    return lax.all_to_all(
        jnp.broadcast_to(value[None], (count,) + value.shape), axes, 0, 0
    )


def weights_kernel(mem_ref, gram_ref, project_ref, out_ref, work):
    blocks, size, members = gram_ref.shape
    shape = (size, members)
    own = out_ref.shape[0]
    lane = lax.broadcasted_iota(jnp.int32, shape, 1)
    sub = lax.broadcasted_iota(jnp.int32, shape, 0)
    slabs = [
        gram_ref[k] + jnp.where(lane == sub + k * size, 1.0, 0.0) for k in range(blocks)
    ]
    slabs.append(jnp.broadcast_to(project_ref[...], shape))
    for k in range(blocks):
        base = k * size
        inside = (lane >= base) & (lane < base + size)
        slab = slabs[k]
        columns = [
            jnp.broadcast_to(slab[:, base + c : base + c + 1], shape) for c in range(size)
        ]
        entry = {
            (c, r): jnp.broadcast_to(columns[c][r : r + 1], shape)
            for c in range(size)
            for r in range(c, size)
        }
        start = jnp.where(inside, jnp.where(lane == sub + base, 1.0, 0.0), slab)
        rows = [jnp.broadcast_to(start[r : r + 1], shape) for r in range(size)]
        scales = []
        for j in range(size):
            scale = lax.rsqrt(entry[j, j])
            scales.append(scale)
            rows[j] = rows[j] * scale
            for i in range(j + 1, size):
                entry[j, i] = entry[j, i] * scale
            for i in range(j + 1, size):
                rows[i] = rows[i] - entry[j, i] * rows[j]
                for c in range(i, size):
                    entry[i, c] = entry[i, c] - entry[j, i] * entry[j, c]
        for i in range(k + 1, blocks + 1):
            target = slabs[i]
            kept = jnp.where(inside, 0.0, target)
            factors = []
            for j in range(size):
                value = jnp.broadcast_to(target[:, base + j : base + j + 1], shape)
                for c in range(j):
                    value = value - factors[c] * entry[c, j]
                value = value * scales[j]
                factors.append(value)
                kept = kept - value * rows[j]
            slabs[i] = kept
        final = rows[0]
        for r in range(1, size):
            final = jnp.where(sub == r, rows[r], final)
        slabs[k] = jnp.where(lane < base + size, final, 0.0)
    shift = slabs[blocks] * (-1.0 / (members - 1) ** 0.5)
    for k in range(blocks):
        combined = slabs[k] + shift
        mean = jnp.sum(combined, axis=1, keepdims=True) * (1.0 / members)
        work[k * size : (k + 1) * size, :] = combined - mean + 1.0 / members
    first = pl.multiple_of(mem_ref[0] * own, own)
    turn = lax.rem(members - first, members)
    out_ref[...] = pltpu.roll(work[pl.ds(first, own), :], turn, 1)


def analysis_weights(mem_index, gram, project, own):
    members = gram.shape[2]
    return pl.pallas_call(
        weights_kernel,
        out_shape=jax.ShapeDtypeStruct((own, members), jnp.float32),
        in_specs=[
            pl.BlockSpec(memory_space=pltpu.SMEM),
            pl.BlockSpec(memory_space=pltpu.VMEM),
            pl.BlockSpec(memory_space=pltpu.VMEM),
        ],
        out_specs=pl.BlockSpec(memory_space=pltpu.VMEM),
        scratch_shapes=[pltpu.VMEM((members, members), jnp.float32)],
    )(mem_index.reshape(1), gram, project)


def mix_kernel(weights_ref, *refs):
    *sources, pair_ref, speed_ref = refs
    kinds, depth, members, width = sources[0].shape
    weights = weights_ref[...]
    high = weights.astype(jnp.bfloat16)
    low = (weights - high.astype(jnp.float32)).astype(jnp.bfloat16)
    both = jnp.concatenate([high, low], axis=0)
    for kind in range(kinds):
        for row in range(0, depth, 2):
            tile = jnp.concatenate(
                [
                    jnp.concatenate(
                        [source[kind, row + i] for source in sources], axis=0
                    )
                    for i in range(2)
                ],
                axis=1,
            )
            tile_high = tile.astype(jnp.bfloat16)
            tile_low = (tile - tile_high.astype(jnp.float32)).astype(jnp.bfloat16)
            main = jnp.dot(both, tile_high, preferred_element_type=jnp.float32)
            rest = jnp.dot(high, tile_low, preferred_element_type=jnp.float32)
            result = main[:members] + (main[members:] + rest)
            for i in range(2):
                part = result[:, i * width : (i + 1) * width]
                if kind < 2:
                    pair_ref[:, kind, row + i, :] = part
                else:
                    speed_ref[:, row + i, :] = part


def mix(weights, sources):
    groups = len(sources)
    kinds, depth, members, width = sources[0].shape
    return pl.pallas_call(
        mix_kernel,
        grid=(2,),
        in_specs=[
            pl.BlockSpec((members, groups * members), lambda i: (0, 0)),
        ]
        + [pl.BlockSpec((kinds, depth // 2, members, width), lambda i: (0, i, 0, 0))] * groups,
        out_specs=[
            pl.BlockSpec((members, 2, depth // 2, width), lambda i: (0, 0, i, 0)),
            pl.BlockSpec((members, depth // 2, width), lambda i: (0, i, 0)),
        ],
        out_shape=[
            jax.ShapeDtypeStruct((members, 2, depth, width), jnp.float32),
            jax.ShapeDtypeStruct((members, depth, width), jnp.float32),
        ],
        compiler_params=pltpu.CompilerParams(vmem_limit_bytes=24 * 1024 * 1024),
    )(weights, *sources)


def on_device(member_heat_solute, velocity, phase_mask, obs_index, obs_value, obs_error):
    members, _, depth, width = member_heat_solute.shape
    mushy = phase_mask.astype(jnp.float32)
    count = lax.axis_size(SPACE)
    position = lax.axis_index(SPACE)

    def edge(first):
        rows = slice(first, first + 2)
        return jnp.concatenate(
            [
                member_heat_solute[:, 0, rows],
                member_heat_solute[:, 1, rows],
                velocity[:, rows],
                mushy[None, rows],
            ],
            axis=0,
        )

    above = lax.ppermute(edge(depth - 2), SPACE, [(i, i + 1) for i in range(count - 1)])
    below = lax.ppermute(edge(0), SPACE, [(i + 1, i) for i in range(count - 1)])
    fields = jnp.concatenate(
        [member_heat_solute[:, 0], member_heat_solute[:, 1], velocity, mushy[None]], axis=0
    )
    padded = jnp.concatenate([above, fields, below], axis=1)
    mushy = padded[3 * members]
    factor = 1.0 - mushy * (1.0 - mushy_ratio)
    heat = padded[:members]
    solute = padded[members : 2 * members]
    speed = padded[2 * members : 3 * members]
    heat, solute, speed = advance(heat, solute, speed, mushy, factor)
    row = lax.broadcasted_iota(jnp.int32, (depth + 2, 1), 0)
    outside = ((row == 0) & (position == 0)) | ((row == depth + 1) & (position == count - 1))
    heat = jnp.where(outside, 0.0, heat)
    solute = jnp.where(outside, 0.0, solute)
    speed = jnp.where(outside, 0.0, speed)
    heat, solute, speed = advance(heat, solute, speed, mushy[1:-1], factor[1:-1])

    temp = heat * factor[2:-2]
    flat_temp = temp.reshape(members, -1)
    cell_ids = jnp.arange(flat_temp.shape[1], dtype=jnp.int32)
    selector = jnp.where(obs_index[:, None] == cell_ids[None, :], 1.0, 0.0).astype(jnp.float32)
    observed_own = jnp.dot(selector, flat_temp.T, precision=HIGHEST)
    message = jnp.concatenate([observed_own, obs_value[:, None], obs_error[:, None]], axis=1)
    arrived = shared(message, ("y", "core", "mem"))
    mem_size = lax.axis_size("mem")
    slabs = arrived.shape[0] // mem_size
    n_obs = message.shape[0]
    arrived = arrived.reshape(slabs, mem_size, n_obs, members + 2)
    ensemble = mem_size * members
    measured = arrived[..., :members].transpose(0, 2, 1, 3).reshape(slabs * n_obs, ensemble)
    value = arrived[:, 0, :, members].reshape(slabs * n_obs)
    error = arrived[:, 0, :, members + 1].reshape(slabs * n_obs)
    mean_obs = jnp.mean(measured, axis=1)
    spread = (measured - mean_obs[:, None]) / (
        error[:, None] * jnp.sqrt(jnp.float32(ensemble - 1))
    )
    innovation = (value - mean_obs) / error
    pieces = lax.axis_size(("y", "core"))
    piece = lax.axis_index(("y", "core"))
    height = ensemble // pieces
    own_cols = lax.dynamic_slice_in_dim(spread, piece * height, height, 1)
    left = jnp.concatenate([own_cols, innovation[:, None]], axis=1)
    part = lax.dot_general(left, spread, (((0,), (0,)), ((), ())), precision=HIGHEST)
    part = jnp.sum(shared(part, "z"), axis=0)
    project = part[height:]
    gram = shared(part[:height], ("y", "core"))
    mem_index = lax.axis_index("mem")
    weights = analysis_weights(mem_index, gram, project, members)
    states = jnp.stack([heat, solute, speed], axis=0).transpose(0, 2, 1, 3)
    sources = [states]
    for step in range(1, mem_size):
        pairs = [((i + step) % mem_size, i) for i in range(mem_size)]
        sources.append(lax.ppermute(states, "mem", pairs))
    return mix(weights, sources)


def solution(mesh):
    shaped = Mesh(mesh.devices.reshape(16, 8, 2, 4), ("z", "y", "core", "mem"))
    return jax.shard_map(
        on_device,
        mesh=shaped,
        in_specs=(
            P("mem", None, SPACE, None),
            P("mem", SPACE, None),
            P(SPACE, None),
            P(SPACE),
            P(SPACE),
            P(SPACE),
        ),
        out_specs=(P("mem", None, SPACE, None), P("mem", SPACE, None)),
        check_vma=False,
    )
```

```python
import jax
import jax.numpy as jnp
from jax import lax
from jax.experimental import pallas as pl
from jax.experimental.pallas import tpu as pltpu
from jax.sharding import Mesh
from jax.sharding import PartitionSpec as P

heat_diffusion = 0.15
advection = 0.4
solute_diffusion = 0.05
segregation = 0.3
momentum_diffusion = 0.1
darcy_drag = 0.5
mushy_ratio = 1.0 / 3.0

SPACE = ("z", "y", "core")
HIGHEST = lax.Precision.HIGHEST


def lateral(field, lane):
    last = field.shape[1] - 1
    left = jnp.where(lane == 0, field, pltpu.roll(field, 1, 1))
    right = jnp.where(lane == last, field, pltpu.roll(field, last, 1))
    return left + right - 2.0 * field


def advance(heat, temp, solute, speed, mushy, lane):
    def laplacian(rows):
        return rows[2] + rows[0] - 2.0 * rows[1] + lateral(rows[1], lane)

    carried = advection * speed[1]
    new_heat = heat[1] + heat_diffusion * laplacian(temp) - carried * (heat[1] - heat[0])
    new_solute = (
        solute[1]
        + solute_diffusion * laplacian(solute)
        - carried * (solute[1] - solute[0])
        + segregation * mushy * (temp[1] - solute[1])
    )
    new_speed = speed[1] + momentum_diffusion * laplacian(speed) - darcy_drag * mushy * speed[1]
    return new_heat, new_solute, new_speed


def edge_kernel(pair_ref, speed_ref, mask_ref, tail_ref, head_ref):
    depth = mask_ref.shape[0]
    members = speed_ref.shape[0] // depth
    for out_ref, first in ((tail_ref, depth - 2), (head_ref, 0)):
        for i in range(2):
            row = first + i
            for kind in range(3):
                if kind < 2:
                    part = pair_ref[pl.ds(kind * depth + row, members, stride=2 * depth), :]
                else:
                    part = speed_ref[pl.ds(row, members, stride=depth), :]
                place = (i * 3 + kind) * members
                out_ref[place : place + members, :] = part
        place = 6 * members
        out_ref[place : place + 8, :] = jnp.zeros((8, out_ref.shape[1]), jnp.float32)
        out_ref[place : place + 2, :] = mask_ref[first : first + 2, :].astype(jnp.float32)


def edges(pair, speed, mask):
    members = speed.shape[0] // mask.shape[0]
    shape = jax.ShapeDtypeStruct((6 * members + 8, mask.shape[1]), jnp.float32)
    return pl.pallas_call(edge_kernel, out_shape=[shape, shape])(pair, speed, mask)


def forecast_kernel(
    ends_ref, index_ref, value_ref, error_ref, pair_ref, speed_ref, mask_ref, above_ref,
    below_ref, states_ref, message_ref, middle, temps
):
    depth, width = mask_ref.shape
    members = states_ref.shape[2]
    n_obs = index_ref.shape[0]
    lane = lax.broadcasted_iota(jnp.int32, (members, width), 1)

    def outer(kind, row):
        if row < 0:
            place = ((row + 2) * 3 + kind) * members
            return above_ref[place : place + members, :]
        if row >= depth:
            place = ((row - depth) * 3 + kind) * members
            return below_ref[place : place + members, :]
        if kind < 2:
            return pair_ref[pl.ds(kind * depth + row, members, stride=2 * depth), :]
        return speed_ref[pl.ds(row, members, stride=depth), :]

    def mushy_at(row):
        place = 6 * members
        if row < 0:
            return above_ref[place + row + 2 : place + row + 3, :]
        if row >= depth:
            return below_ref[place + row - depth : place + row - depth + 1, :]
        return mask_ref[row : row + 1, :].astype(jnp.float32)

    def inner(kind, row):
        return middle[kind, row + 1]

    mushy = {row: mushy_at(row) for row in range(-2, depth + 2)}
    factor = {row: 1.0 - m * (1.0 - mushy_ratio) for row, m in mushy.items()}

    def sweep(get, first, last, put):
        heat = {r: get(0, r) for r in (first - 1, first)}
        solute = {r: get(1, r) for r in (first - 1, first)}
        speed = {r: get(2, r) for r in (first - 1, first)}
        temp = {r: heat[r] * factor[r] for r in heat}
        for row in range(first, last):
            heat[row + 1] = get(0, row + 1)
            solute[row + 1] = get(1, row + 1)
            speed[row + 1] = get(2, row + 1)
            temp[row + 1] = heat[row + 1] * factor[row + 1]
            near = range(row - 1, row + 2)
            put(
                row,
                advance(
                    [heat[r] for r in near],
                    [temp[r] for r in near],
                    [solute[r] for r in near],
                    [speed[r] for r in near],
                    mushy[row],
                    lane,
                ),
            )

    def keep(row, new):
        for kind in range(3):
            part = new[kind]
            if row < 0:
                part = jnp.where(ends_ref[0] == 1, 0.0, part)
            if row >= depth:
                part = jnp.where(ends_ref[1] == 1, 0.0, part)
            middle[kind, row + 1] = part

    def finish(row, new):
        for kind in range(3):
            states_ref[kind, row] = new[kind]
        temps[row] = new[0] * factor[row]

    sweep(outer, -1, depth + 1, keep)
    sweep(inner, 0, depth, finish)

    root = float(4 * members - 1) ** 0.5
    seen = jnp.zeros((members, width), jnp.float32)
    for o in range(n_obs):
        cell = index_ref[o]
        tile = temps[cell // width]
        column = jnp.sum(jnp.where(lane == cell % width, tile, 0.0), axis=1, keepdims=True)
        scale = jnp.full((members, 1), error_ref[o], jnp.float32) * root
        place = (o // 4) * 8 + o % 4
        seen = jnp.where(lane == place, (column - value_ref[o]) / scale, seen)
    square = jnp.concatenate(
        [seen, jnp.zeros((width - members, width), jnp.float32)], axis=0
    ).T
    packed = square[0:8]
    for q in range(1, n_obs // 4):
        packed = packed + pltpu.roll(square[q * 8 : q * 8 + 8], q * members, 1)
    for peer in range(message_ref.shape[0]):
        message_ref[peer] = packed[0:4]


def forecast(ends, obs_index, obs_value, obs_error, pair, speed, mask, above, below, peers):
    depth, width = mask.shape
    members = speed.shape[0] // depth
    scalar = pl.BlockSpec(memory_space=pltpu.SMEM)
    whole = pl.BlockSpec(memory_space=pltpu.VMEM)
    return pl.pallas_call(
        forecast_kernel,
        in_specs=[scalar] * 4 + [whole] * 5,
        out_specs=[whole, whole],
        out_shape=[
            jax.ShapeDtypeStruct((3, depth, members, width), jnp.float32),
            jax.ShapeDtypeStruct((peers, 4, width), jnp.float32),
        ],
        scratch_shapes=[
            pltpu.VMEM((3, depth + 2, members, width), jnp.float32),
            pltpu.VMEM((depth, members, width), jnp.float32),
        ],
        compiler_params=pltpu.CompilerParams(vmem_limit_bytes=24 * 1024 * 1024),
    )(ends, obs_index, obs_value, obs_error, pair, speed, mask, above, below)


def gram_kernel(piece_ref, arrived_ref, states_ref, out_ref, passed_ref, work):
    del states_ref, passed_ref
    total, width = arrived_ref.shape
    slabs = total // 16
    share = width // 4
    lane = lax.broadcasted_iota(jnp.int32, (slabs, width), 1)
    blocks = []
    for a in range(4):
        held = [arrived_ref[pl.ds(m * 4 + a, slabs, stride=16), :] for m in range(4)]
        for q in range(4):
            block = pltpu.roll(held[0], (-q * share) % width, 1) if q else held[0]
            for m in range(1, 4):
                turn = ((m - q) * share) % width
                part = pltpu.roll(held[m], turn, 1) if turn else held[m]
                block = jnp.where(lane // share == m, part, block)
            blocks.append(block)
    scaled = jnp.concatenate(blocks, axis=0)
    mean = jnp.sum(scaled, axis=1, keepdims=True) * (1.0 / width)
    spread = scaled - mean
    innovation = mean * -(float(width - 1) ** 0.5)
    work[...] = lax.dot_general(
        spread, spread, (((0,), (0,)), ((), ())), precision=HIGHEST,
        preferred_element_type=jnp.float32,
    )
    project = jnp.sum(spread * innovation, axis=0, keepdims=True)
    height = out_ref.shape[1] - 1
    first = piece_ref[0] * height
    for r in range(height):
        row = work[pl.ds(first + r, 1), :]
        for i in range(out_ref.shape[0]):
            out_ref[i, r] = row
    for i in range(out_ref.shape[0]):
        out_ref[i, height] = project


def gram_part(piece, arrived, states, peers, height):
    width = arrived.shape[1]
    return pl.pallas_call(
        gram_kernel,
        in_specs=[
            pl.BlockSpec(memory_space=pltpu.SMEM),
            pl.BlockSpec(memory_space=pltpu.VMEM),
            pl.BlockSpec(memory_space=pl.ANY),
        ],
        out_specs=[
            pl.BlockSpec(memory_space=pltpu.VMEM),
            pl.BlockSpec(memory_space=pl.ANY),
        ],
        out_shape=[
            jax.ShapeDtypeStruct((peers, height + 1, 1, width), jnp.float32),
            jax.ShapeDtypeStruct(states.shape, jnp.float32),
        ],
        input_output_aliases={2: 1},
        scratch_shapes=[pltpu.VMEM((width, width), jnp.float32)],
    )(piece.reshape(1), arrived, states)


def total_kernel(parts_ref, piece_ref, project_ref, work):
    count, rows = parts_ref.shape[:2]
    for r in range(rows):
        row = parts_ref[0, r]
        for i in range(1, count):
            row = row + parts_ref[i, r]
        if r < rows - 1:
            work[r : r + 1, :] = row
        else:
            project_ref[...] = row
    piece = work[...]
    for i in range(piece_ref.shape[0]):
        piece_ref[i] = piece


def total(parts, peers):
    rows, width = parts.shape[1] - 1, parts.shape[3]
    return pl.pallas_call(
        total_kernel,
        out_shape=[
            jax.ShapeDtypeStruct((peers, rows, width), jnp.float32),
            jax.ShapeDtypeStruct((1, width), jnp.float32),
        ],
        scratch_shapes=[pltpu.VMEM((rows, width), jnp.float32)],
    )(parts)


def weights_kernel(mem_ref, gram_ref, project_ref, out_ref, work):
    blocks, size, members = gram_ref.shape
    shape = (size, members)
    own = out_ref.shape[0]
    lane = lax.broadcasted_iota(jnp.int32, shape, 1)
    sub = lax.broadcasted_iota(jnp.int32, shape, 0)
    slabs = [
        gram_ref[k] + jnp.where(lane == sub + k * size, 1.0, 0.0) for k in range(blocks)
    ]
    slabs.append(jnp.broadcast_to(project_ref[...], shape))
    for k in range(blocks):
        base = k * size
        inside = (lane >= base) & (lane < base + size)
        slab = slabs[k]
        columns = [
            jnp.broadcast_to(slab[:, base + c : base + c + 1], shape) for c in range(size)
        ]
        entry = {
            (c, r): jnp.broadcast_to(columns[c][r : r + 1], shape)
            for c in range(size)
            for r in range(c, size)
        }
        start = jnp.where(inside, jnp.where(lane == sub + base, 1.0, 0.0), slab)
        rows = [jnp.broadcast_to(start[r : r + 1], shape) for r in range(size)]
        scales = []
        for j in range(size):
            scale = lax.rsqrt(entry[j, j])
            scales.append(scale)
            rows[j] = rows[j] * scale
            for i in range(j + 1, size):
                entry[j, i] = entry[j, i] * scale
            for i in range(j + 1, size):
                rows[i] = rows[i] - entry[j, i] * rows[j]
                for c in range(i, size):
                    entry[i, c] = entry[i, c] - entry[j, i] * entry[j, c]
        for i in range(k + 1, blocks + 1):
            target = slabs[i]
            kept = jnp.where(inside, 0.0, target)
            factors = []
            for j in range(size):
                value = jnp.broadcast_to(target[:, base + j : base + j + 1], shape)
                for c in range(j):
                    value = value - factors[c] * entry[c, j]
                value = value * scales[j]
                factors.append(value)
                kept = kept - value * rows[j]
            slabs[i] = kept
        final = rows[0]
        for r in range(1, size):
            final = jnp.where(sub == r, rows[r], final)
        slabs[k] = jnp.where(lane < base + size, final, 0.0)
    shift = slabs[blocks] * (-1.0 / (members - 1) ** 0.5)
    for k in range(blocks):
        combined = slabs[k] + shift
        mean = jnp.sum(combined, axis=1, keepdims=True) * (1.0 / members)
        work[k * size : (k + 1) * size, :] = combined - mean + 1.0 / members
    first = pl.multiple_of(mem_ref[0] * own, own)
    turn = lax.rem(members - first, members)
    out_ref[...] = pltpu.roll(work[pl.ds(first, own), :], turn, 1)


def analysis_weights(mem_index, gram, project, own):
    members = gram.shape[2]
    return pl.pallas_call(
        weights_kernel,
        out_shape=jax.ShapeDtypeStruct((own, members), jnp.float32),
        in_specs=[
            pl.BlockSpec(memory_space=pltpu.SMEM),
            pl.BlockSpec(memory_space=pltpu.VMEM),
            pl.BlockSpec(memory_space=pltpu.VMEM),
        ],
        out_specs=pl.BlockSpec(memory_space=pltpu.VMEM),
        scratch_shapes=[pltpu.VMEM((members, members), jnp.float32)],
    )(mem_index.reshape(1), gram, project)


def mix_kernel(weights_ref, *refs):
    *sources, pair_ref, speed_ref = refs
    kinds, depth, members, width = sources[0].shape
    weights = weights_ref[...]
    high = weights.astype(jnp.bfloat16)
    low = (weights - high.astype(jnp.float32)).astype(jnp.bfloat16)
    both = jnp.concatenate([high, low], axis=0)
    for kind in range(kinds):
        for row in range(0, depth, 2):
            tile = jnp.concatenate(
                [
                    jnp.concatenate(
                        [source[kind, row + i] for source in sources], axis=0
                    )
                    for i in range(2)
                ],
                axis=1,
            )
            tile_high = tile.astype(jnp.bfloat16)
            tile_low = (tile - tile_high.astype(jnp.float32)).astype(jnp.bfloat16)
            main = jnp.dot(both, tile_high, preferred_element_type=jnp.float32)
            rest = jnp.dot(high, tile_low, preferred_element_type=jnp.float32)
            result = main[:members] + (main[members:] + rest)
            for i in range(2):
                part = result[:, i * width : (i + 1) * width]
                if kind < 2:
                    pair_ref[:, kind, row + i, :] = part
                else:
                    speed_ref[:, row + i, :] = part


def mix(weights, sources):
    groups = len(sources)
    kinds, depth, members, width = sources[0].shape
    return pl.pallas_call(
        mix_kernel,
        grid=(2,),
        in_specs=[
            pl.BlockSpec((members, groups * members), lambda i: (0, 0)),
        ]
        + [pl.BlockSpec((kinds, depth // 2, members, width), lambda i: (0, i, 0, 0))] * groups,
        out_specs=[
            pl.BlockSpec((members, 2, depth // 2, width), lambda i: (0, 0, i, 0)),
            pl.BlockSpec((members, depth // 2, width), lambda i: (0, i, 0)),
        ],
        out_shape=[
            jax.ShapeDtypeStruct((members, 2, depth, width), jnp.float32),
            jax.ShapeDtypeStruct((members, depth, width), jnp.float32),
        ],
        compiler_params=pltpu.CompilerParams(vmem_limit_bytes=24 * 1024 * 1024),
    )(weights, *sources)


def on_device(member_heat_solute, velocity, phase_mask, obs_index, obs_value, obs_error):
    members, _, depth, width = member_heat_solute.shape
    pair = member_heat_solute.reshape(members * 2 * depth, width)
    speed = velocity.reshape(members * depth, width)
    count = lax.axis_size(SPACE)
    position = lax.axis_index(SPACE)
    ends = jnp.stack([position == 0, position == count - 1]).astype(jnp.int32)
    tail, head = edges(pair, speed, phase_mask)
    above = lax.ppermute(tail, SPACE, [(i, i + 1) for i in range(count - 1)])
    below = lax.ppermute(head, SPACE, [(i + 1, i) for i in range(count - 1)])
    group = ("y", "core", "mem")
    states, message = forecast(
        ends, obs_index, obs_value, obs_error, pair, speed, phase_mask, above, below,
        lax.axis_size(group),
    )
    arrived = lax.all_to_all(message, group, 0, 0)
    arrived = arrived.reshape(-1, width)
    mem_size = lax.axis_size("mem")
    pieces = lax.axis_size(("y", "core"))
    part, states = gram_part(
        lax.axis_index(("y", "core")), arrived, states, lax.axis_size("z"), mem_size * members // pieces
    )
    part = lax.all_to_all(part, "z", 0, 0)
    piece, project = total(part, pieces)
    gram = lax.all_to_all(piece, ("y", "core"), 0, 0)
    mem_index = lax.axis_index("mem")
    weights = analysis_weights(mem_index, gram, project, members)
    sources = [states]
    for step in range(1, mem_size):
        pairs = [((i + step) % mem_size, i) for i in range(mem_size)]
        sources.append(lax.ppermute(states, "mem", pairs))
    return mix(weights, sources)


def solution(mesh):
    shaped = Mesh(mesh.devices.reshape(16, 8, 2, 4), ("z", "y", "core", "mem"))
    return jax.shard_map(
        on_device,
        mesh=shaped,
        in_specs=(
            P("mem", None, SPACE, None),
            P("mem", SPACE, None),
            P(SPACE, None),
            P(SPACE),
            P(SPACE),
            P(SPACE),
        ),
        out_specs=(P("mem", None, SPACE, None), P("mem", SPACE, None)),
        check_vma=False,
    )
```

```python
import jax
import jax.numpy as jnp
from jax import lax
from jax.experimental import pallas as pl
from jax.experimental.pallas import tpu as pltpu
from jax.sharding import Mesh
from jax.sharding import PartitionSpec as P

heat_diffusion = 0.15
advection = 0.4
solute_diffusion = 0.05
segregation = 0.3
momentum_diffusion = 0.1
darcy_drag = 0.5
mushy_ratio = 1.0 / 3.0

SPACE = ("z", "y", "core")
HIGHEST = lax.Precision.HIGHEST


def lateral(field, lane):
    last = field.shape[1] - 1
    left = jnp.where(lane == 0, field, pltpu.roll(field, 1, 1))
    right = jnp.where(lane == last, field, pltpu.roll(field, last, 1))
    return left + right - 2.0 * field


def advance(heat, temp, solute, speed, mushy, lane):
    def laplacian(rows):
        return rows[2] + rows[0] - 2.0 * rows[1] + lateral(rows[1], lane)

    carried = advection * speed[1]
    new_heat = heat[1] + heat_diffusion * laplacian(temp) - carried * (heat[1] - heat[0])
    new_solute = (
        solute[1]
        + solute_diffusion * laplacian(solute)
        - carried * (solute[1] - solute[0])
        + segregation * mushy * (temp[1] - solute[1])
    )
    new_speed = speed[1] + momentum_diffusion * laplacian(speed) - darcy_drag * mushy * speed[1]
    return new_heat, new_solute, new_speed


def edge_kernel(pair_ref, speed_ref, mask_ref, tail_ref, head_ref):
    depth = mask_ref.shape[0]
    members = speed_ref.shape[0] // depth
    for out_ref, first in ((tail_ref, depth - 2), (head_ref, 0)):
        for i in range(2):
            row = first + i
            for kind in range(3):
                if kind < 2:
                    part = pair_ref[pl.ds(kind * depth + row, members, stride=2 * depth), :]
                else:
                    part = speed_ref[pl.ds(row, members, stride=depth), :]
                place = (i * 3 + kind) * members
                out_ref[place : place + members, :] = part
        place = 6 * members
        out_ref[place : place + 8, :] = jnp.zeros((8, out_ref.shape[1]), jnp.float32)
        out_ref[place : place + 2, :] = mask_ref[first : first + 2, :].astype(jnp.float32)


def edges(pair, speed, mask):
    members = speed.shape[0] // mask.shape[0]
    shape = jax.ShapeDtypeStruct((6 * members + 8, mask.shape[1]), jnp.float32)
    return pl.pallas_call(edge_kernel, out_shape=[shape, shape])(pair, speed, mask)


def forecast_kernel(
    ends_ref, index_ref, value_ref, error_ref, pair_ref, speed_ref, mask_ref, above_ref,
    below_ref, states_ref, message_ref, middle, temps
):
    depth, width = mask_ref.shape
    members = states_ref.shape[2]
    n_obs = index_ref.shape[0]
    lane = lax.broadcasted_iota(jnp.int32, (members, width), 1)

    def outer(kind, row):
        if row < 0:
            place = ((row + 2) * 3 + kind) * members
            return above_ref[place : place + members, :]
        if row >= depth:
            place = ((row - depth) * 3 + kind) * members
            return below_ref[place : place + members, :]
        if kind < 2:
            return pair_ref[pl.ds(kind * depth + row, members, stride=2 * depth), :]
        return speed_ref[pl.ds(row, members, stride=depth), :]

    def mushy_at(row):
        place = 6 * members
        if row < 0:
            return above_ref[place + row + 2 : place + row + 3, :]
        if row >= depth:
            return below_ref[place + row - depth : place + row - depth + 1, :]
        return mask_ref[row : row + 1, :].astype(jnp.float32)

    def inner(kind, row):
        return middle[kind, row + 1]

    mushy = {row: mushy_at(row) for row in range(-2, depth + 2)}
    factor = {row: 1.0 - m * (1.0 - mushy_ratio) for row, m in mushy.items()}

    def sweep(get, first, last, put):
        heat = {r: get(0, r) for r in (first - 1, first)}
        solute = {r: get(1, r) for r in (first - 1, first)}
        speed = {r: get(2, r) for r in (first - 1, first)}
        temp = {r: heat[r] * factor[r] for r in heat}
        for row in range(first, last):
            heat[row + 1] = get(0, row + 1)
            solute[row + 1] = get(1, row + 1)
            speed[row + 1] = get(2, row + 1)
            temp[row + 1] = heat[row + 1] * factor[row + 1]
            near = range(row - 1, row + 2)
            put(
                row,
                advance(
                    [heat[r] for r in near],
                    [temp[r] for r in near],
                    [solute[r] for r in near],
                    [speed[r] for r in near],
                    mushy[row],
                    lane,
                ),
            )

    def keep(row, new):
        for kind in range(3):
            part = new[kind]
            if row < 0:
                part = jnp.where(ends_ref[0] == 1, 0.0, part)
            if row >= depth:
                part = jnp.where(ends_ref[1] == 1, 0.0, part)
            middle[kind, row + 1] = part

    def finish(row, new):
        for kind in range(3):
            states_ref[kind, row] = new[kind]
        temps[row] = new[0] * factor[row]

    sweep(outer, -1, depth + 1, keep)
    sweep(inner, 0, depth, finish)

    root = float(4 * members - 1) ** 0.5
    seen = jnp.zeros((members, width), jnp.float32)
    for o in range(n_obs):
        cell = index_ref[o]
        tile = temps[cell // width]
        column = jnp.sum(jnp.where(lane == cell % width, tile, 0.0), axis=1, keepdims=True)
        scale = jnp.full((members, 1), error_ref[o], jnp.float32) * root
        place = (o // 4) * 8 + o % 4
        seen = jnp.where(lane == place, (column - value_ref[o]) / scale, seen)
    square = jnp.concatenate(
        [seen, jnp.zeros((width - members, width), jnp.float32)], axis=0
    ).T
    packed = square[0:8]
    for q in range(1, n_obs // 4):
        packed = packed + pltpu.roll(square[q * 8 : q * 8 + 8], q * members, 1)
    for peer in range(message_ref.shape[0]):
        message_ref[peer] = packed[0:4]


def forecast(ends, obs_index, obs_value, obs_error, pair, speed, mask, above, below, peers):
    depth, width = mask.shape
    members = speed.shape[0] // depth
    scalar = pl.BlockSpec(memory_space=pltpu.SMEM)
    whole = pl.BlockSpec(memory_space=pltpu.VMEM)
    return pl.pallas_call(
        forecast_kernel,
        in_specs=[scalar] * 4 + [whole] * 5,
        out_specs=[whole, whole],
        out_shape=[
            jax.ShapeDtypeStruct((3, depth, members, width), jnp.float32),
            jax.ShapeDtypeStruct((peers, 4, width), jnp.float32),
        ],
        scratch_shapes=[
            pltpu.VMEM((3, depth + 2, members, width), jnp.float32),
            pltpu.VMEM((depth, members, width), jnp.float32),
        ],
        compiler_params=pltpu.CompilerParams(vmem_limit_bytes=24 * 1024 * 1024),
    )(ends, obs_index, obs_value, obs_error, pair, speed, mask, above, below)


def gram_kernel(piece_ref, arrived_ref, out_ref, work):
    total, width = arrived_ref.shape
    slabs = total // 16
    share = width // 4
    lane = lax.broadcasted_iota(jnp.int32, (slabs, width), 1)
    blocks = []
    for a in range(4):
        held = [arrived_ref[pl.ds(m * 4 + a, slabs, stride=16), :] for m in range(4)]
        for q in range(4):
            block = pltpu.roll(held[0], (-q * share) % width, 1) if q else held[0]
            for m in range(1, 4):
                turn = ((m - q) * share) % width
                part = pltpu.roll(held[m], turn, 1) if turn else held[m]
                block = jnp.where(lane // share == m, part, block)
            blocks.append(block)
    scaled = jnp.concatenate(blocks, axis=0)
    mean = jnp.sum(scaled, axis=1, keepdims=True) * (1.0 / width)
    spread = scaled - mean
    innovation = mean * -(float(width - 1) ** 0.5)
    work[...] = lax.dot_general(
        spread, spread, (((0,), (0,)), ((), ())), precision=HIGHEST,
        preferred_element_type=jnp.float32,
    )
    project = jnp.sum(spread * innovation, axis=0, keepdims=True)
    height = out_ref.shape[1] - 1
    first = piece_ref[0] * height
    for r in range(height):
        row = work[pl.ds(first + r, 1), :]
        for i in range(out_ref.shape[0]):
            out_ref[i, r] = row
    for i in range(out_ref.shape[0]):
        out_ref[i, height] = project


def gram_part(piece, arrived, peers, height):
    width = arrived.shape[1]
    return pl.pallas_call(
        gram_kernel,
        in_specs=[
            pl.BlockSpec(memory_space=pltpu.SMEM),
            pl.BlockSpec(memory_space=pltpu.VMEM),
        ],
        out_specs=pl.BlockSpec(memory_space=pltpu.VMEM),
        out_shape=jax.ShapeDtypeStruct((peers, height + 1, 1, width), jnp.float32),
        scratch_shapes=[pltpu.VMEM((width, width), jnp.float32)],
        cost_estimate=pl.CostEstimate(
            flops=10_000_000_000, bytes_accessed=1_000_000, transcendentals=0
        ),
    )(piece.reshape(1), arrived)


def total_kernel(parts_ref, piece_ref, project_ref, work):
    count, rows = parts_ref.shape[:2]
    for r in range(rows):
        row = parts_ref[0, r]
        for i in range(1, count):
            row = row + parts_ref[i, r]
        if r < rows - 1:
            work[r : r + 1, :] = row
        else:
            project_ref[...] = row
    piece = work[...]
    for i in range(piece_ref.shape[0]):
        piece_ref[i] = piece


def total(parts, peers):
    rows, width = parts.shape[1] - 1, parts.shape[3]
    return pl.pallas_call(
        total_kernel,
        out_shape=[
            jax.ShapeDtypeStruct((peers, rows, width), jnp.float32),
            jax.ShapeDtypeStruct((1, width), jnp.float32),
        ],
        scratch_shapes=[pltpu.VMEM((rows, width), jnp.float32)],
    )(parts)


def weights_kernel(mem_ref, gram_ref, project_ref, out_ref, work):
    blocks, size, members = gram_ref.shape
    shape = (size, members)
    own = out_ref.shape[0]
    lane = lax.broadcasted_iota(jnp.int32, shape, 1)
    sub = lax.broadcasted_iota(jnp.int32, shape, 0)
    slabs = [
        gram_ref[k] + jnp.where(lane == sub + k * size, 1.0, 0.0) for k in range(blocks)
    ]
    slabs.append(jnp.broadcast_to(project_ref[...], shape))
    for k in range(blocks):
        base = k * size
        inside = (lane >= base) & (lane < base + size)
        slab = slabs[k]
        columns = [
            jnp.broadcast_to(slab[:, base + c : base + c + 1], shape) for c in range(size)
        ]
        entry = {
            (c, r): jnp.broadcast_to(columns[c][r : r + 1], shape)
            for c in range(size)
            for r in range(c, size)
        }
        start = jnp.where(inside, jnp.where(lane == sub + base, 1.0, 0.0), slab)
        rows = [jnp.broadcast_to(start[r : r + 1], shape) for r in range(size)]
        scales = []
        for j in range(size):
            scale = lax.rsqrt(entry[j, j])
            scales.append(scale)
            rows[j] = rows[j] * scale
            for i in range(j + 1, size):
                entry[j, i] = entry[j, i] * scale
            for i in range(j + 1, size):
                rows[i] = rows[i] - entry[j, i] * rows[j]
                for c in range(i, size):
                    entry[i, c] = entry[i, c] - entry[j, i] * entry[j, c]
        for i in range(k + 1, blocks + 1):
            target = slabs[i]
            kept = jnp.where(inside, 0.0, target)
            factors = []
            for j in range(size):
                value = jnp.broadcast_to(target[:, base + j : base + j + 1], shape)
                for c in range(j):
                    value = value - factors[c] * entry[c, j]
                value = value * scales[j]
                factors.append(value)
                kept = kept - value * rows[j]
            slabs[i] = kept
        final = rows[0]
        for r in range(1, size):
            final = jnp.where(sub == r, rows[r], final)
        slabs[k] = jnp.where(lane < base + size, final, 0.0)
    shift = slabs[blocks] * (-1.0 / (members - 1) ** 0.5)
    for k in range(blocks):
        combined = slabs[k] + shift
        mean = jnp.sum(combined, axis=1, keepdims=True) * (1.0 / members)
        work[k * size : (k + 1) * size, :] = combined - mean + 1.0 / members
    first = pl.multiple_of(mem_ref[0] * own, own)
    turn = lax.rem(members - first, members)
    out_ref[...] = pltpu.roll(work[pl.ds(first, own), :], turn, 1)


def analysis_weights(mem_index, gram, project, own):
    members = gram.shape[2]
    return pl.pallas_call(
        weights_kernel,
        out_shape=jax.ShapeDtypeStruct((own, members), jnp.float32),
        in_specs=[
            pl.BlockSpec(memory_space=pltpu.SMEM),
            pl.BlockSpec(memory_space=pltpu.VMEM),
            pl.BlockSpec(memory_space=pltpu.VMEM),
        ],
        out_specs=pl.BlockSpec(memory_space=pltpu.VMEM),
        scratch_shapes=[pltpu.VMEM((members, members), jnp.float32)],
    )(mem_index.reshape(1), gram, project)


def mix_kernel(weights_ref, *refs):
    *sources, pair_ref, speed_ref = refs
    kinds, depth, members, width = sources[0].shape
    weights = weights_ref[...]
    high = weights.astype(jnp.bfloat16)
    low = (weights - high.astype(jnp.float32)).astype(jnp.bfloat16)
    both = jnp.concatenate([high, low], axis=0)
    for kind in range(kinds):
        for row in range(0, depth, 2):
            tile = jnp.concatenate(
                [
                    jnp.concatenate(
                        [source[kind, row + i] for source in sources], axis=0
                    )
                    for i in range(2)
                ],
                axis=1,
            )
            tile_high = tile.astype(jnp.bfloat16)
            tile_low = (tile - tile_high.astype(jnp.float32)).astype(jnp.bfloat16)
            main = jnp.dot(both, tile_high, preferred_element_type=jnp.float32)
            rest = jnp.dot(high, tile_low, preferred_element_type=jnp.float32)
            result = main[:members] + (main[members:] + rest)
            for i in range(2):
                part = result[:, i * width : (i + 1) * width]
                if kind < 2:
                    pair_ref[:, kind, row + i, :] = part
                else:
                    speed_ref[:, row + i, :] = part


def mix(weights, sources):
    groups = len(sources)
    kinds, depth, members, width = sources[0].shape
    return pl.pallas_call(
        mix_kernel,
        grid=(2,),
        in_specs=[
            pl.BlockSpec((members, groups * members), lambda i: (0, 0)),
        ]
        + [pl.BlockSpec((kinds, depth // 2, members, width), lambda i: (0, i, 0, 0))] * groups,
        out_specs=[
            pl.BlockSpec((members, 2, depth // 2, width), lambda i: (0, 0, i, 0)),
            pl.BlockSpec((members, depth // 2, width), lambda i: (0, i, 0)),
        ],
        out_shape=[
            jax.ShapeDtypeStruct((members, 2, depth, width), jnp.float32),
            jax.ShapeDtypeStruct((members, depth, width), jnp.float32),
        ],
        compiler_params=pltpu.CompilerParams(vmem_limit_bytes=24 * 1024 * 1024),
    )(weights, *sources)


def on_device(member_heat_solute, velocity, phase_mask, obs_index, obs_value, obs_error):
    members, _, depth, width = member_heat_solute.shape
    pair = member_heat_solute.reshape(members * 2 * depth, width)
    speed = velocity.reshape(members * depth, width)
    count = lax.axis_size(SPACE)
    position = lax.axis_index(SPACE)
    ends = jnp.stack([position == 0, position == count - 1]).astype(jnp.int32)
    tail, head = edges(pair, speed, phase_mask)
    above = lax.ppermute(tail, SPACE, [(i, i + 1) for i in range(count - 1)])
    below = lax.ppermute(head, SPACE, [(i + 1, i) for i in range(count - 1)])
    group = ("y", "core", "mem")
    states, message = forecast(
        ends, obs_index, obs_value, obs_error, pair, speed, phase_mask, above, below,
        lax.axis_size(group),
    )
    arrived = lax.all_to_all(message, group, 0, 0)
    arrived = arrived.reshape(-1, width)
    mem_size = lax.axis_size("mem")
    pieces = lax.axis_size(("y", "core"))
    part = gram_part(
        lax.axis_index(("y", "core")), arrived, lax.axis_size("z"), mem_size * members // pieces
    )
    part = lax.all_to_all(part, "z", 0, 0)
    piece, project = total(part, pieces)
    gram = lax.all_to_all(piece, ("y", "core"), 0, 0)
    mem_index = lax.axis_index("mem")
    weights = analysis_weights(mem_index, gram, project, members)
    sources = [states]
    for step in range(1, mem_size):
        pairs = [((i + step) % mem_size, i) for i in range(mem_size)]
        sources.append(lax.ppermute(states, "mem", pairs))
    return mix(weights, sources)


def solution(mesh):
    shaped = Mesh(mesh.devices.reshape(16, 8, 2, 4), ("z", "y", "core", "mem"))
    return jax.shard_map(
        on_device,
        mesh=shaped,
        in_specs=(
            P("mem", None, SPACE, None),
            P("mem", SPACE, None),
            P(SPACE, None),
            P(SPACE),
            P(SPACE),
            P(SPACE),
        ),
        out_specs=(P("mem", None, SPACE, None), P("mem", SPACE, None)),
        check_vma=False,
    )
```

```python
import jax
import jax.numpy as jnp
from jax import lax
from jax.experimental import pallas as pl
from jax.experimental.pallas import tpu as pltpu
from jax.sharding import Mesh
from jax.sharding import PartitionSpec as P

heat_diffusion = 0.15
advection = 0.4
solute_diffusion = 0.05
segregation = 0.3
momentum_diffusion = 0.1
darcy_drag = 0.5
mushy_ratio = 1.0 / 3.0

SPACE = ("z", "y", "core")
HIGHEST = lax.Precision.HIGHEST


def lateral(field, lane):
    last = field.shape[1] - 1
    left = jnp.where(lane == 0, field, pltpu.roll(field, 1, 1))
    right = jnp.where(lane == last, field, pltpu.roll(field, last, 1))
    return left + right - 2.0 * field


def advance(heat, temp, solute, speed, mushy, lane):
    def laplacian(rows):
        return rows[2] + rows[0] - 2.0 * rows[1] + lateral(rows[1], lane)

    carried = advection * speed[1]
    new_heat = heat[1] + heat_diffusion * laplacian(temp) - carried * (heat[1] - heat[0])
    new_solute = (
        solute[1]
        + solute_diffusion * laplacian(solute)
        - carried * (solute[1] - solute[0])
        + segregation * mushy * (temp[1] - solute[1])
    )
    new_speed = speed[1] + momentum_diffusion * laplacian(speed) - darcy_drag * mushy * speed[1]
    return new_heat, new_solute, new_speed


def edge_kernel(pair_ref, speed_ref, mask_ref, tail_ref, head_ref):
    depth = mask_ref.shape[0]
    members = speed_ref.shape[0] // depth
    for out_ref, first in ((tail_ref, depth - 2), (head_ref, 0)):
        for i in range(2):
            row = first + i
            for kind in range(3):
                if kind < 2:
                    part = pair_ref[pl.ds(kind * depth + row, members, stride=2 * depth), :]
                else:
                    part = speed_ref[pl.ds(row, members, stride=depth), :]
                place = (i * 3 + kind) * members
                out_ref[place : place + members, :] = part
        place = 6 * members
        out_ref[place : place + 8, :] = jnp.zeros((8, out_ref.shape[1]), jnp.float32)
        out_ref[place : place + 2, :] = mask_ref[first : first + 2, :].astype(jnp.float32)


def edges(pair, speed, mask):
    members = speed.shape[0] // mask.shape[0]
    shape = jax.ShapeDtypeStruct((6 * members + 8, mask.shape[1]), jnp.float32)
    return pl.pallas_call(edge_kernel, out_shape=[shape, shape])(pair, speed, mask)


def forecast_kernel(
    ends_ref, index_ref, value_ref, error_ref, pair_ref, speed_ref, mask_ref, above_ref,
    below_ref, states_ref, message_ref, middle, temps
):
    depth, width = mask_ref.shape
    members = states_ref.shape[2]
    n_obs = index_ref.shape[0]
    lane = lax.broadcasted_iota(jnp.int32, (members, width), 1)

    def outer(kind, row):
        if row < 0:
            place = ((row + 2) * 3 + kind) * members
            return above_ref[place : place + members, :]
        if row >= depth:
            place = ((row - depth) * 3 + kind) * members
            return below_ref[place : place + members, :]
        if kind < 2:
            return pair_ref[pl.ds(kind * depth + row, members, stride=2 * depth), :]
        return speed_ref[pl.ds(row, members, stride=depth), :]

    def mushy_at(row):
        place = 6 * members
        if row < 0:
            return above_ref[place + row + 2 : place + row + 3, :]
        if row >= depth:
            return below_ref[place + row - depth : place + row - depth + 1, :]
        return mask_ref[row : row + 1, :].astype(jnp.float32)

    def inner(kind, row):
        return middle[kind, row + 1]

    mushy = {row: mushy_at(row) for row in range(-2, depth + 2)}
    factor = {row: 1.0 - m * (1.0 - mushy_ratio) for row, m in mushy.items()}

    def sweep(get, first, last, put):
        heat = {r: get(0, r) for r in (first - 1, first)}
        solute = {r: get(1, r) for r in (first - 1, first)}
        speed = {r: get(2, r) for r in (first - 1, first)}
        temp = {r: heat[r] * factor[r] for r in heat}
        for row in range(first, last):
            heat[row + 1] = get(0, row + 1)
            solute[row + 1] = get(1, row + 1)
            speed[row + 1] = get(2, row + 1)
            temp[row + 1] = heat[row + 1] * factor[row + 1]
            near = range(row - 1, row + 2)
            put(
                row,
                advance(
                    [heat[r] for r in near],
                    [temp[r] for r in near],
                    [solute[r] for r in near],
                    [speed[r] for r in near],
                    mushy[row],
                    lane,
                ),
            )

    def keep(row, new):
        for kind in range(3):
            part = new[kind]
            if row < 0:
                part = jnp.where(ends_ref[0] == 1, 0.0, part)
            if row >= depth:
                part = jnp.where(ends_ref[1] == 1, 0.0, part)
            middle[kind, row + 1] = part

    def finish(row, new):
        for kind in range(3):
            states_ref[kind, row] = new[kind]
        temps[row] = new[0] * factor[row]

    sweep(outer, -1, depth + 1, keep)
    sweep(inner, 0, depth, finish)

    root = float(4 * members - 1) ** 0.5
    seen = jnp.zeros((members, width), jnp.float32)
    for o in range(n_obs):
        cell = index_ref[o]
        tile = temps[cell // width]
        column = jnp.sum(jnp.where(lane == cell % width, tile, 0.0), axis=1, keepdims=True)
        scale = jnp.full((members, 1), error_ref[o], jnp.float32) * root
        place = (o // 4) * 8 + o % 4
        seen = jnp.where(lane == place, (column - value_ref[o]) / scale, seen)
    square = jnp.concatenate(
        [seen, jnp.zeros((width - members, width), jnp.float32)], axis=0
    ).T
    packed = square[0:8]
    for q in range(1, n_obs // 4):
        packed = packed + pltpu.roll(square[q * 8 : q * 8 + 8], q * members, 1)
    for peer in range(message_ref.shape[0]):
        message_ref[peer] = packed[0:4]


def forecast(ends, obs_index, obs_value, obs_error, pair, speed, mask, above, below, peers):
    depth, width = mask.shape
    members = speed.shape[0] // depth
    scalar = pl.BlockSpec(memory_space=pltpu.SMEM)
    whole = pl.BlockSpec(memory_space=pltpu.VMEM)
    return pl.pallas_call(
        forecast_kernel,
        in_specs=[scalar] * 4 + [whole] * 5,
        out_specs=[whole, whole],
        out_shape=[
            jax.ShapeDtypeStruct((3, depth, members, width), jnp.float32),
            jax.ShapeDtypeStruct((peers, 4, width), jnp.float32),
        ],
        scratch_shapes=[
            pltpu.VMEM((3, depth + 2, members, width), jnp.float32),
            pltpu.VMEM((depth, members, width), jnp.float32),
        ],
        compiler_params=pltpu.CompilerParams(vmem_limit_bytes=24 * 1024 * 1024),
    )(ends, obs_index, obs_value, obs_error, pair, speed, mask, above, below)


def gram_kernel(piece_ref, arrived_ref, out_ref, work):
    total, width = arrived_ref.shape
    slabs = total // 16
    share = width // 4
    lane = lax.broadcasted_iota(jnp.int32, (slabs, width), 1)
    blocks = []
    for a in range(4):
        held = [arrived_ref[pl.ds(m * 4 + a, slabs, stride=16), :] for m in range(4)]
        for q in range(4):
            block = pltpu.roll(held[0], (-q * share) % width, 1) if q else held[0]
            for m in range(1, 4):
                turn = ((m - q) * share) % width
                part = pltpu.roll(held[m], turn, 1) if turn else held[m]
                block = jnp.where(lane // share == m, part, block)
            blocks.append(block)
    scaled = jnp.concatenate(blocks, axis=0)
    mean = jnp.sum(scaled, axis=1, keepdims=True) * (1.0 / width)
    spread = scaled - mean
    innovation = mean * -(float(width - 1) ** 0.5)
    work[...] = lax.dot_general(
        spread, spread, (((0,), (0,)), ((), ())), precision=HIGHEST,
        preferred_element_type=jnp.float32,
    )
    project = jnp.sum(spread * innovation, axis=0, keepdims=True)
    height = out_ref.shape[1] - 1
    first = piece_ref[0] * height
    for r in range(height):
        row = work[pl.ds(first + r, 1), :]
        for i in range(out_ref.shape[0]):
            out_ref[i, r] = row
    for i in range(out_ref.shape[0]):
        out_ref[i, height] = project


def gram_part(piece, arrived, peers, height):
    width = arrived.shape[1]
    return pl.pallas_call(
        gram_kernel,
        in_specs=[
            pl.BlockSpec(memory_space=pltpu.SMEM),
            pl.BlockSpec(memory_space=pltpu.VMEM),
        ],
        out_specs=pl.BlockSpec(memory_space=pltpu.VMEM),
        out_shape=jax.ShapeDtypeStruct((peers, height + 1, 1, width), jnp.float32),
        scratch_shapes=[pltpu.VMEM((width, width), jnp.float32)],
        cost_estimate=pl.CostEstimate(
            flops=10_000_000_000, bytes_accessed=1_000_000, transcendentals=0
        ),
    )(piece.reshape(1), arrived)


def total_kernel(parts_ref, piece_ref, project_ref, work):
    count, rows = parts_ref.shape[:2]
    for r in range(rows):
        row = parts_ref[0, r]
        for i in range(1, count):
            row = row + parts_ref[i, r]
        if r < rows - 1:
            work[r : r + 1, :] = row
        else:
            project_ref[...] = row
    piece = work[...]
    for i in range(piece_ref.shape[0]):
        piece_ref[i] = piece


def total(parts, peers):
    rows, width = parts.shape[1] - 1, parts.shape[3]
    return pl.pallas_call(
        total_kernel,
        out_shape=[
            jax.ShapeDtypeStruct((peers, rows, width), jnp.float32),
            jax.ShapeDtypeStruct((1, width), jnp.float32),
        ],
        scratch_shapes=[pltpu.VMEM((rows, width), jnp.float32)],
    )(parts)


def weights_kernel(mem_ref, gram_ref, project_ref, out_ref, work):
    blocks, size, members = gram_ref.shape
    shape = (size, members)
    own = out_ref.shape[0]
    lane = lax.broadcasted_iota(jnp.int32, shape, 1)
    sub = lax.broadcasted_iota(jnp.int32, shape, 0)
    slabs = [
        gram_ref[k] + jnp.where(lane == sub + k * size, 1.0, 0.0) for k in range(blocks)
    ]
    slabs.append(jnp.broadcast_to(project_ref[...], shape))
    for k in range(blocks):
        base = k * size
        inside = (lane >= base) & (lane < base + size)
        slab = slabs[k]
        columns = [
            jnp.broadcast_to(slab[:, base + c : base + c + 1], shape) for c in range(size)
        ]
        entry = {
            (c, r): jnp.broadcast_to(columns[c][r : r + 1], shape)
            for c in range(size)
            for r in range(c, size)
        }
        start = jnp.where(inside, jnp.where(lane == sub + base, 1.0, 0.0), slab)
        rows = [jnp.broadcast_to(start[r : r + 1], shape) for r in range(size)]
        scales = []
        for j in range(size):
            scale = lax.rsqrt(entry[j, j])
            scales.append(scale)
            rows[j] = rows[j] * scale
            for i in range(j + 1, size):
                entry[j, i] = entry[j, i] * scale
            for i in range(j + 1, size):
                rows[i] = rows[i] - entry[j, i] * rows[j]
                for c in range(i, size):
                    entry[i, c] = entry[i, c] - entry[j, i] * entry[j, c]
        for i in range(k + 1, blocks + 1):
            target = slabs[i]
            kept = jnp.where(inside, 0.0, target)
            factors = []
            for j in range(size):
                value = jnp.broadcast_to(target[:, base + j : base + j + 1], shape)
                for c in range(j):
                    value = value - factors[c] * entry[c, j]
                value = value * scales[j]
                factors.append(value)
                kept = kept - value * rows[j]
            slabs[i] = kept
        final = rows[0]
        for r in range(1, size):
            final = jnp.where(sub == r, rows[r], final)
        slabs[k] = jnp.where(lane < base + size, final, 0.0)
    shift = slabs[blocks] * (-1.0 / (members - 1) ** 0.5)
    for k in range(blocks):
        combined = slabs[k] + shift
        mean = jnp.sum(combined, axis=1, keepdims=True) * (1.0 / members)
        work[k * size : (k + 1) * size, :] = combined - mean + 1.0 / members
    first = pl.multiple_of(mem_ref[0] * own, own)
    turn = lax.rem(members - first, members)
    out_ref[...] = pltpu.roll(work[pl.ds(first, own), :], turn, 1)


def mix_kernel(weights_ref, *refs):
    *sources, pair_ref, speed_ref = refs
    kinds, depth, members, width = sources[0].shape
    weights = weights_ref[...]
    high = weights.astype(jnp.bfloat16)
    low = (weights - high.astype(jnp.float32)).astype(jnp.bfloat16)
    both = jnp.concatenate([high, low], axis=0)
    for kind in range(kinds):
        for row in range(0, depth, 2):
            tile = jnp.concatenate(
                [
                    jnp.concatenate(
                        [source[kind, row + i] for source in sources], axis=0
                    )
                    for i in range(2)
                ],
                axis=1,
            )
            tile_high = tile.astype(jnp.bfloat16)
            tile_low = (tile - tile_high.astype(jnp.float32)).astype(jnp.bfloat16)
            main = jnp.dot(both, tile_high, preferred_element_type=jnp.float32)
            rest = jnp.dot(high, tile_low, preferred_element_type=jnp.float32)
            result = main[:members] + (main[members:] + rest)
            for i in range(2):
                part = result[:, i * width : (i + 1) * width]
                if kind < 2:
                    pair_ref[:, kind, row + i, :] = part
                else:
                    speed_ref[:, row + i, :] = part


def analysis_kernel(mem_ref, gram_ref, project_ref, *refs):
    *blocks, work, weights = refs

    @pl.when(pl.program_id(0) == 0)
    def _():
        weights_kernel(mem_ref, gram_ref, project_ref, weights, work)

    mix_kernel(weights, *blocks)


def analysis(mem_index, gram, project, sources):
    groups = len(sources)
    kinds, depth, members, width = sources[0].shape
    ensemble = groups * members
    return pl.pallas_call(
        analysis_kernel,
        grid=(2,),
        in_specs=[
            pl.BlockSpec(memory_space=pltpu.SMEM),
            pl.BlockSpec(gram.shape, lambda i: (0, 0, 0)),
            pl.BlockSpec(project.shape, lambda i: (0, 0)),
        ]
        + [pl.BlockSpec((kinds, depth // 2, members, width), lambda i: (0, i, 0, 0))] * groups,
        out_specs=[
            pl.BlockSpec((members, 2, depth // 2, width), lambda i: (0, 0, i, 0)),
            pl.BlockSpec((members, depth // 2, width), lambda i: (0, i, 0)),
        ],
        out_shape=[
            jax.ShapeDtypeStruct((members, 2, depth, width), jnp.float32),
            jax.ShapeDtypeStruct((members, depth, width), jnp.float32),
        ],
        scratch_shapes=[
            pltpu.VMEM((ensemble, ensemble), jnp.float32),
            pltpu.VMEM((members, ensemble), jnp.float32),
        ],
        compiler_params=pltpu.CompilerParams(vmem_limit_bytes=24 * 1024 * 1024),
    )(mem_index.reshape(1), gram, project, *sources)


def on_device(member_heat_solute, velocity, phase_mask, obs_index, obs_value, obs_error):
    members, _, depth, width = member_heat_solute.shape
    pair = member_heat_solute.reshape(members * 2 * depth, width)
    speed = velocity.reshape(members * depth, width)
    count = lax.axis_size(SPACE)
    position = lax.axis_index(SPACE)
    ends = jnp.stack([position == 0, position == count - 1]).astype(jnp.int32)
    tail, head = edges(pair, speed, phase_mask)
    above = lax.ppermute(tail, SPACE, [(i, i + 1) for i in range(count - 1)])
    below = lax.ppermute(head, SPACE, [(i + 1, i) for i in range(count - 1)])
    group = ("y", "core", "mem")
    states, message = forecast(
        ends, obs_index, obs_value, obs_error, pair, speed, phase_mask, above, below,
        lax.axis_size(group),
    )
    arrived = lax.all_to_all(message, group, 0, 0)
    arrived = arrived.reshape(-1, width)
    mem_size = lax.axis_size("mem")
    pieces = lax.axis_size(("y", "core"))
    part = gram_part(
        lax.axis_index(("y", "core")), arrived, lax.axis_size("z"), mem_size * members // pieces
    )
    part = lax.all_to_all(part, "z", 0, 0)
    piece, project = total(part, pieces)
    gram = lax.all_to_all(piece, ("y", "core"), 0, 0)
    mem_index = lax.axis_index("mem")
    sources = [states]
    for step in range(1, mem_size):
        pairs = [((i + step) % mem_size, i) for i in range(mem_size)]
        sources.append(lax.ppermute(states, "mem", pairs))
    return analysis(mem_index, gram, project, sources)


def solution(mesh):
    shaped = Mesh(mesh.devices.reshape(16, 8, 2, 4), ("z", "y", "core", "mem"))
    return jax.shard_map(
        on_device,
        mesh=shaped,
        in_specs=(
            P("mem", None, SPACE, None),
            P("mem", SPACE, None),
            P(SPACE, None),
            P(SPACE),
            P(SPACE),
            P(SPACE),
        ),
        out_specs=(P("mem", None, SPACE, None), P("mem", SPACE, None)),
        check_vma=False,
    )
```
